32 devices in a mesh: ctx: 16 (over z, y, x), kv: 2 (over core).
Axes of the slice: x: 2, y: 2, z: 4, core: 2. Of those that a mesh axis runs over, the one named last changes fastest.
Arguments:
- queries: bfloat16 [4096, 2048], P(('ctx', 'kv')), may hold values from -27 to 27
- key_states: bfloat16 [4096, 256], P(('ctx', 'kv')), may hold values from -12 to 12
- value_states: bfloat16 [4096, 256], P(('ctx', 'kv')), may hold values from -6 to 6
- out_grad: bfloat16 [4096, 2048], P(('ctx', 'kv')), may hold values from -6 to 6
- doc_lengths: int32 [8], replicated, may hold values from 1 to 1024, 4096 in all
Outputs:
- attention: bfloat16 [4096, 2048], P(('ctx', 'kv'))
- query_grad: bfloat16 [4096, 2048], P(('ctx', 'kv'))
- key_grad: bfloat16 [4096, 256], P(('ctx', 'kv'))
- value_grad: bfloat16 [4096, 256], P(('ctx', 'kv'))
The draws below stay inside these ranges and needn't reach their ends.
Inputs may be any that keep to these rules, and one draw needn't show every extreme that they name: `doc_lengths`: the lengths sum to 4096; the largest is exactly 1024.
All inputs are finite; a program needn't handle non-finite values.
Results may differ from the reference program's by a relative error of at most 0.018.
Values may be sent and summed in bfloat16 or wider, within the bound.
A program may use at most 64 MiB of HBM per device.

```python
import math
import jax
import jax.numpy as jnp
import numpy as np
from jax import lax

QHEADS = 16
KVHEADS = 2
HEAD_DIM = 128
DOC_MAX = 1024
TOK_DEV = 256
TOKENS = 4096
DOCS = 8
REACH = 4
N_CTX = 16


def draw_queries(key, part):
    key = jax.random.fold_in(key, 1)
    return jnp.clip(jax.random.normal(key, (TOKENS, QHEADS * HEAD_DIM), jnp.float32), -6.0, 6.0).astype(jnp.bfloat16)


def draw_key_states(key, part):
    key = jax.random.fold_in(key, 2)
    return jnp.clip(jax.random.normal(key, (TOKENS, KVHEADS * HEAD_DIM), jnp.float32), -6.0, 6.0).astype(jnp.bfloat16)


def block_scale(own_key, shape, shards, low, top_value):
    def one(position, shards_of):
        heights = jax.random.uniform(jax.random.fold_in(jax.random.fold_in(own_key, 6), position), (shards_of,), jnp.float32, low / len(shards), top_value / len(shards))
        return jnp.repeat(jnp.exp(heights), shape[position] // shards_of).reshape((-1,) + (1,) * (len(shape) - position - 1))

    loudness = one(*shards[0])
    for cut in shards[1:]:
        loudness = loudness * one(*cut)
    return loudness


def profile(number_of, total, most, skew):
    weights = [(1 << 20) // math.isqrt(grade ** skew) + 1 for grade in range(2, number_of + 1)]
    surplus, given = total - most - (number_of - 1), [1] * (number_of - 1)
    while surplus > 0:
        candidates = [i for i in range(number_of - 1) if given[i] < most]
        mass, budget = sum([weights[i] for i in candidates]), surplus
        for i in candidates:
            addition = min(most - given[i], max(1, budget * weights[i] // mass), surplus)
            given[i] = given[i] + addition
            surplus = surplus - addition
    return np.array([most] + given)


def uneven(own_key, number_of, total, reach, skew):
    if number_of == 2:
        one = jax.random.randint(own_key, (), max(1, total - reach), min(reach, total - 1) + 1)
        return jnp.stack([one, total - one])
    tallies = jnp.asarray(profile(number_of, total, reach, skew), jnp.int32)
    twos = (number_of - 1) // 2
    donor, taker = tallies[1:1 + 2 * twos:2], tallies[2:2 + 2 * twos:2]
    slack = jnp.minimum(donor - 1, reach - taker)
    moved = jax.random.randint(jax.random.fold_in(own_key, 1), (twos,), 0, 1 << 20) % (slack + 1)
    tallies = tallies.at[1:1 + 2 * twos:2].set(donor - moved).at[2:2 + 2 * twos:2].set(taker + moved)
    return tallies[jax.random.permutation(jax.random.fold_in(own_key, 2), number_of)]


def centred(stream_key, dims, spread, bound, pieces=(), kind=jnp.bfloat16):
    result = spread * jax.random.normal(stream_key, dims, jnp.float32)
    if pieces:
        result = result * block_scale(stream_key, dims, pieces, -0.22, 0.18)
    return jnp.clip(result, -bound, bound).astype(kind)


def setup_inputs(seed: int = 0) -> dict:
    key_list = jax.random.split(jax.random.key(seed), 6)
    queries = draw_queries(jax.random.fold_in(key_list[5], 71), 0)
    key_states = draw_key_states(jax.random.fold_in(key_list[5], 71), 0)
    value_states = centred(key_list[2], (TOKENS, KVHEADS * HEAD_DIM), 1.0, 6.0, ((0, 32),))
    out_grad = centred(key_list[3], (TOKENS, QHEADS * HEAD_DIM), 1.0, 6.0, ((0, 32),))
    doc_lengths = uneven(key_list[4], DOCS, TOKENS, DOC_MAX, 1).astype(jnp.int32)
    return dict(queries=queries, key_states=key_states, value_states=value_states, out_grad=out_grad, doc_lengths=doc_lengths)


def doc_index(positions, doc_ends):
    return lax.optimization_barrier(jnp.sum((doc_ends[None, :] <= positions[:, None]).astype(jnp.int32), axis=1))

def block_mask(first_row, doc_ends):
    query_pos = first_row + jnp.arange(TOK_DEV, dtype=jnp.int32)
    key_pos = first_row - REACH * TOK_DEV + jnp.arange((REACH + 1) * TOK_DEV, dtype=jnp.int32)
    same_doc = doc_index(query_pos, doc_ends)[:, None] == doc_index(key_pos, doc_ends)[None, :]
    return same_doc & (key_pos[None, :] <= query_pos[:, None]) & (key_pos[None, :] >= 0)

def block_terms(query_block, grad_block, key_window, value_window, allowed):
    factor = 1.0 / math.sqrt(HEAD_DIM)
    per_group = QHEADS // KVHEADS
    window_rows = key_window.shape[0]

    def one_head(totals, head_id):
        key_acc, value_acc = totals
        column = head_id // per_group * HEAD_DIM
        query_rows = lax.dynamic_slice_in_dim(query_block, head_id * HEAD_DIM, HEAD_DIM, 1)
        grad_rows = lax.dynamic_slice_in_dim(grad_block, head_id * HEAD_DIM, HEAD_DIM, 1)
        key_cols = lax.dynamic_slice_in_dim(key_window, column, HEAD_DIM, 1)
        value_cols = lax.dynamic_slice_in_dim(value_window, column, HEAD_DIM, 1)
        scores = jnp.dot(query_rows, key_cols.T, preferred_element_type=jnp.float32) * factor
        highest = lax.optimization_barrier(jnp.max(jnp.where(allowed, scores, -jnp.inf), axis=1, keepdims=True))
        expsum = lax.optimization_barrier(jnp.sum(jnp.where(allowed, jnp.exp(scores - highest), 0.0), axis=1, keepdims=True))
        log_total = highest + jnp.log(expsum)
        prob_rows = jnp.where(allowed, jnp.exp(scores - log_total), 0.0)
        probs_low = prob_rows.astype(jnp.bfloat16)
        output = jnp.dot(probs_low, value_cols, preferred_element_type=jnp.float32).astype(jnp.bfloat16)
        row_dot = lax.optimization_barrier(jnp.sum(grad_rows.astype(jnp.float32) * output.astype(jnp.float32), axis=1, keepdims=True))
        grad_probs = jnp.dot(grad_rows, value_cols.T, preferred_element_type=jnp.float32)
        grad_scores = (prob_rows * (grad_probs - row_dot)).astype(jnp.bfloat16)
        query_grad = (jnp.dot(grad_scores, key_cols, preferred_element_type=jnp.float32) * factor).astype(jnp.bfloat16)
        key_term = jnp.dot(grad_scores.T, query_rows, preferred_element_type=jnp.float32) * factor
        value_term = jnp.dot(probs_low.T, grad_rows, preferred_element_type=jnp.float32)
        key_acc = lax.dynamic_update_slice_in_dim(key_acc, lax.dynamic_slice_in_dim(key_acc, column, HEAD_DIM, 1) + key_term, column, 1)
        value_acc = lax.dynamic_update_slice_in_dim(value_acc, lax.dynamic_slice_in_dim(value_acc, column, HEAD_DIM, 1) + value_term, column, 1)
        return ((key_acc, value_acc), (output, query_grad))
    zeros_acc = jnp.zeros((window_rows, KVHEADS * HEAD_DIM), jnp.float32)
    (key_acc, value_acc), (outputs, query_grads) = lax.scan(one_head, (zeros_acc, zeros_acc), jnp.arange(QHEADS, dtype=jnp.int32))
    attention = jnp.moveaxis(outputs, 0, 1).reshape(TOK_DEV, QHEADS * HEAD_DIM)
    query_grad = jnp.moveaxis(query_grads, 0, 1).reshape(TOK_DEV, QHEADS * HEAD_DIM)
    return (attention, query_grad, key_acc, value_acc)

def fold_parts(parts):
    tiles = parts.reshape(N_CTX, REACH + 1, TOK_DEV, parts.shape[-1])
    totals = jnp.zeros((N_CTX + REACH, TOK_DEV, parts.shape[-1]), jnp.float32)
    for tile_index in range(REACH + 1):
        totals = totals.at[tile_index:tile_index + N_CTX].add(tiles[:, tile_index])
    return totals[REACH:].reshape(TOKENS, parts.shape[-1]).astype(jnp.bfloat16)

def reference(queries, key_states, value_states, out_grad, doc_lengths):
    doc_ends = jnp.cumsum(doc_lengths).astype(jnp.int32)
    front = REACH * TOK_DEV
    key_padded = jnp.concatenate([jnp.zeros((front, key_states.shape[1]), key_states.dtype), key_states], axis=0)
    value_padded = jnp.concatenate([jnp.zeros((front, value_states.shape[1]), value_states.dtype), value_states], axis=0)

    def per_block(block_id):
        first_row = block_id * TOK_DEV
        query_block = lax.dynamic_slice_in_dim(queries, first_row, TOK_DEV, 0)
        grad_block = lax.dynamic_slice_in_dim(out_grad, first_row, TOK_DEV, 0)
        key_window = lax.dynamic_slice_in_dim(key_padded, first_row, front + TOK_DEV, 0)
        value_window = lax.dynamic_slice_in_dim(value_padded, first_row, front + TOK_DEV, 0)
        allowed = block_mask(first_row, doc_ends)
        return block_terms(query_block, grad_block, key_window, value_window, allowed)
    attention, query_grad, key_parts, value_parts = lax.map(per_block, jnp.arange(N_CTX, dtype=jnp.int32))
    attention = attention.reshape(TOKENS, QHEADS * HEAD_DIM)
    query_grad = query_grad.reshape(TOKENS, QHEADS * HEAD_DIM)
    return (attention, query_grad, fold_parts(key_parts), fold_parts(value_parts))
```

```python
import functools
import math

import jax
import jax.numpy as jnp
from jax import lax
from jax.experimental import pallas as pl
from jax.experimental.pallas import tpu as pltpu
from jax.sharding import PartitionSpec as P

HEAD_DIM = 128
DOC_MAX = 1024
MESH = pl.DeviceIdType.MESH


def dot_last(left, right):
    return lax.dot_general(
        left, right, (((1,), (1,)), ((), ())), preferred_element_type=jnp.float32
    )


def dot_plain(left, right):
    return jnp.dot(left, right, preferred_element_type=jnp.float32)


def kernel(
    n_ctx, reach, heads,
    q_hbm, g_hbm, k_hbm, v_hbm, doc_ref,
    att_hbm, dq_hbm, dk_ref, dv_ref,
    qraw, graw, qst, gst, kwin, vwin, kwin_t, vwin_t, bias, probs, dscores,
    part_out, part_in, att_buf, dq_buf,
    load_sem, kv_send, kv_recv, qg_send, qg_recv, part_send, part_recv, out_send, out_recv, out_sem,
):
    c = lax.axis_index("ctx")
    m = lax.axis_index("kv")
    other = 1 - m
    T = k_hbm.shape[0]
    D = HEAD_DIM
    shard = 2 * T
    half_cols = heads * D
    span = reach * shard + T
    factor = 1.0 / math.sqrt(D)

    def later(j):
        return c + j < n_ctx

    def earlier(j):
        return c >= j

    barrier = pltpu.get_barrier_semaphore()
    pl.semaphore_signal(barrier, inc=1, device_id=(c, other), device_id_type=MESH)
    for j in range(1, reach + 1):
        @pl.when(later(j))
        def _():
            for e in range(2):
                pl.semaphore_signal(barrier, inc=1, device_id=(c + j, e), device_id_type=MESH)

        @pl.when(earlier(j))
        def _():
            for e in range(2):
                pl.semaphore_signal(barrier, inc=1, device_id=(c - j, e), device_id_type=MESH)

    own_cols = pl.ds(pl.multiple_of(m * half_cols, D), half_cols)
    own_key_cols = pl.ds(pl.multiple_of(m * D, D), D)
    own_rows = pl.ds(pl.multiple_of(reach * shard + m * T, T), T)
    loads = [
        pltpu.make_async_copy(k_hbm.at[:, own_key_cols], kwin.at[own_rows], load_sem.at[0]),
        pltpu.make_async_copy(v_hbm.at[:, own_key_cols], vwin.at[own_rows], load_sem.at[1]),
        pltpu.make_async_copy(q_hbm.at[:, own_cols], qraw.at[m], load_sem.at[2]),
        pltpu.make_async_copy(g_hbm.at[:, own_cols], graw.at[m], load_sem.at[3]),
    ]
    for copy in loads:
        copy.start()

    peers = jnp.int32(1)
    for j in range(1, reach + 1):
        peers = peers + jnp.where(later(j), 2, 0) + jnp.where(earlier(j), 2, 0)
    pl.semaphore_wait(barrier, peers)

    def kv_copy(j, dest, sender):
        cols = pl.ds(pl.multiple_of(dest * D, D), D)
        rows = pl.ds(pl.multiple_of((reach - j) * shard + sender * T, T), T)
        copies = []
        for which, (src, dst) in enumerate(((k_hbm, kwin), (v_hbm, vwin))):
            copies.append(
                pltpu.make_async_remote_copy(
                    src_ref=src.at[:, cols],
                    dst_ref=dst.at[rows],
                    send_sem=kv_send.at[(j * 2 + dest) * 2 + which],
                    recv_sem=kv_recv.at[(j * 2 + sender) * 2 + which],
                    device_id=(c + j, dest),
                    device_id_type=MESH,
                )
            )
        return copies

    for j in range(reach, 0, -1):
        @pl.when(later(j))
        def _():
            for dest in range(2):
                for copy in kv_copy(j, dest, m):
                    copy.start()
    for copy in kv_copy(0, other, m):
        copy.start()

    def qg_copies(sender, dest):
        cols = pl.ds(pl.multiple_of(dest * half_cols, D), half_cols)
        copies = []
        for which, (src, dst) in enumerate(((q_hbm, qraw), (g_hbm, graw))):
            copies.append(
                pltpu.make_async_remote_copy(
                    src_ref=src.at[:, cols],
                    dst_ref=dst.at[sender],
                    send_sem=qg_send.at[which],
                    recv_sem=qg_recv.at[which],
                    device_id=(c, dest),
                    device_id_type=MESH,
                )
            )
        return copies

    for copy in qg_copies(m, other):
        copy.start()

    for j in range(1, reach + 1):
        @pl.when(jnp.logical_not(earlier(j)))
        def _():
            rows = pl.ds((reach - j) * shard, shard)
            kwin[rows, :] = jnp.zeros((shard, D), kwin.dtype)
            vwin[rows, :] = jnp.zeros((shard, D), vwin.dtype)

        @pl.when(jnp.logical_not(later(j)))
        def _():
            part_in[j] = jnp.zeros(part_in.shape[1:], part_in.dtype)

    for t in range(2):
        row_pos = c * shard + t * T + lax.broadcasted_iota(jnp.int32, (1, T), 1)
        first = jnp.zeros((1, T), jnp.int32)
        end = jnp.int32(0)
        for d in range(doc_ref.shape[0]):
            end = end + doc_ref[d]
            first = jnp.where(end <= row_pos, end, first)
        key_pos = (c - reach) * shard + t * T + lax.broadcasted_iota(jnp.int32, (span, T), 0)
        allowed = (key_pos >= first) & (key_pos <= row_pos)
        bias[t] = jnp.where(allowed, 0.0, -1e30)

    for copy in loads:
        copy.wait()
    for copy in qg_copies(other, m):
        copy.wait_recv()
    for t in range(2):
        for h in range(heads):
            qst[t, h * T : (h + 1) * T, :] = qraw[t, :, h * D : (h + 1) * D]
            gst[t, h * T : (h + 1) * T, :] = graw[t, :, h * D : (h + 1) * D]
    for copy in kv_copy(0, m, other):
        copy.wait_recv()
    for j in range(1, reach + 1):
        @pl.when(earlier(j))
        def _():
            for sender in range(2):
                for copy in kv_copy(j, m, sender):
                    copy.wait_recv()

    kwin_t[...] = kwin[...].T
    vwin_t[...] = vwin[...].T

    pair = 2 * T
    scale2 = factor * math.log2(math.e)

    for t in range(2):
        keys = slice(t * T, t * T + span)

        def one_pair(i, carry):
            cols = pl.ds(pl.multiple_of(i * pair, pair), pair)
            scores = dot_last(kwin[keys, :], qst[t, cols, :])
            mask_term = bias[t]
            z = scores * scale2 + jnp.concatenate([mask_term, mask_term], axis=1)
            highest = jnp.max(z, axis=0, keepdims=True)
            e = jnp.exp2(z - highest)
            total = jnp.sum(e, axis=0, keepdims=True)
            p = e * (1.0 / total)
            gp = dot_last(vwin[keys, :], gst[t, cols, :])
            row_dot = jnp.sum(p * gp, axis=0, keepdims=True)
            probs[t, :, cols] = p.astype(jnp.bfloat16)
            dscores[t, :, cols] = (p * (gp - row_dot)).astype(jnp.bfloat16)
            return carry

        lax.fori_loop(0, heads // 2, one_pair, 0)

    for which, (lhs, rhs, scale) in enumerate(((dscores, qst, factor), (probs, gst, 1.0))):
        low = dot_plain(lhs[0], rhs[0]) * scale
        high = dot_plain(lhs[1], rhs[1]) * scale
        for block in range(2 * (reach + 1)):
            value = None
            if block < 2 * reach + 1:
                value = low[block * T : (block + 1) * T]
            if block >= 1:
                part = high[(block - 1) * T : block * T]
                value = part if value is None else value + part
            part_out[reach - block // 2, block % 2, which] = value.astype(part_out.dtype)

    def part_copy(j, dest, sender):
        return pltpu.make_async_remote_copy(
            src_ref=part_out.at[j, dest],
            dst_ref=part_in.at[j, sender],
            send_sem=part_send.at[j * 2 + dest],
            recv_sem=part_recv.at[j * 2 + sender],
            device_id=(c - j, dest),
            device_id_type=MESH,
        )

    for j in range(reach, 0, -1):
        @pl.when(earlier(j))
        def _():
            for dest in range(2):
                part_copy(j, dest, m).start()
    part_copy(0, other, m).start()

    def remote_out(sender, dest):
        cols = pl.ds(pl.multiple_of(sender * half_cols, D), half_cols)
        return [
            pltpu.make_async_remote_copy(
                src_ref=src.at[dest],
                dst_ref=dst.at[:, cols],
                send_sem=out_send.at[which],
                recv_sem=out_recv.at[which],
                device_id=(c, dest),
                device_id_type=MESH,
            )
            for which, (src, dst) in enumerate(((att_buf, att_hbm), (dq_buf, dq_hbm)))
        ]

    def outputs(t):
        keys = pl.ds(pl.multiple_of(t * T, T), span)

        def one_pair(i, carry):
            cols = pl.ds(pl.multiple_of(i * pair, pair), pair)
            o = dot_plain(vwin_t[:, keys], probs[t, :, cols]).T
            dq = (dot_plain(kwin_t[:, keys], dscores[t, :, cols]) * factor).T
            for a in range(2):
                at = pl.ds(pl.multiple_of(i * 2 * D + a * D, D), D)
                att_buf[t, :, at] = o[a * T : (a + 1) * T].astype(att_buf.dtype)
                dq_buf[t, :, at] = dq[a * T : (a + 1) * T].astype(dq_buf.dtype)
            return carry

        lax.fori_loop(0, heads // 2, one_pair, 0)

    outputs(other)
    for copy in remote_out(m, other):
        copy.start()
    outputs(m)
    stores = [
        pltpu.make_async_copy(att_buf.at[m], att_hbm.at[:, own_cols], out_sem.at[0]),
        pltpu.make_async_copy(dq_buf.at[m], dq_hbm.at[:, own_cols], out_sem.at[1]),
    ]
    for copy in stores:
        copy.start()

    part_in[0, m] = part_out[0, m]
    part_copy(0, m, other).wait_recv()
    for j in range(1, reach + 1):
        @pl.when(later(j))
        def _():
            for sender in range(2):
                part_copy(j, m, sender).wait_recv()
    for which, ref in enumerate((dk_ref, dv_ref)):
        for e in range(2):
            total = part_in[0, e, which].astype(jnp.float32)
            for j in range(1, reach + 1):
                total = total + part_in[j, e, which].astype(jnp.float32)
            ref[:, e * D : (e + 1) * D] = total.astype(ref.dtype)

    for copy in stores:
        copy.wait()
    for copy in remote_out(other, m):
        copy.wait_recv()
    for copy in remote_out(m, other):
        copy.wait_send()
    for copy in qg_copies(m, other):
        copy.wait_send()
    for copy in kv_copy(0, other, m):
        copy.wait_send()
    part_copy(0, other, m).wait_send()
    for j in range(1, reach + 1):
        @pl.when(later(j))
        def _():
            for dest in range(2):
                for copy in kv_copy(j, dest, m):
                    copy.wait_send()

        @pl.when(earlier(j))
        def _():
            for dest in range(2):
                part_copy(j, dest, m).wait_send()


def solution(mesh):
    n_ctx = mesh.shape["ctx"]

    def body(queries, key_states, value_states, out_grad, doc_lengths):
        T, q_cols = queries.shape
        D = HEAD_DIM
        heads = q_cols // D // 2
        shard = 2 * T
        reach = (DOC_MAX - 1) // shard + 1
        window = (reach + 1) * shard
        span = reach * shard + T
        bf16, f32 = jnp.bfloat16, jnp.float32
        hbm = pl.BlockSpec(memory_space=pl.ANY)
        vmem = pl.BlockSpec(memory_space=pltpu.VMEM)
        dma = pltpu.SemaphoreType.DMA
        return pl.pallas_call(
            functools.partial(kernel, n_ctx, reach, heads),
            out_shape=(
                jax.ShapeDtypeStruct(queries.shape, bf16),
                jax.ShapeDtypeStruct(queries.shape, bf16),
                jax.ShapeDtypeStruct(key_states.shape, bf16),
                jax.ShapeDtypeStruct(key_states.shape, bf16),
            ),
            in_specs=[hbm] * 4 + [pl.BlockSpec(memory_space=pltpu.SMEM)],
            out_specs=(hbm, hbm, vmem, vmem),
            scratch_shapes=[
                pltpu.VMEM((2, T, heads * D), bf16),
                pltpu.VMEM((2, T, heads * D), bf16),
                pltpu.VMEM((2, heads * T, D), bf16),
                pltpu.VMEM((2, heads * T, D), bf16),
                pltpu.VMEM((window, D), bf16),
                pltpu.VMEM((window, D), bf16),
                pltpu.VMEM((D, window), bf16),
                pltpu.VMEM((D, window), bf16),
                pltpu.VMEM((2, span, T), f32),
                pltpu.VMEM((2, span, heads * T), bf16),
                pltpu.VMEM((2, span, heads * T), bf16),
                pltpu.VMEM((reach + 1, 2, 2, T, D), bf16),
                pltpu.VMEM((reach + 1, 2, 2, T, D), bf16),
                pltpu.VMEM((2, T, heads * D), bf16),
                pltpu.VMEM((2, T, heads * D), bf16),
                dma((4,)),
                dma(((reach + 1) * 4,)),
                dma(((reach + 1) * 4,)),
                dma((2,)),
                dma((2,)),
                dma(((reach + 1) * 2,)),
                dma(((reach + 1) * 2,)),
                dma((2,)),
                dma((2,)),
                dma((2,)),
            ],
            compiler_params=pltpu.CompilerParams(
                collective_id=0, has_side_effects=True, vmem_limit_bytes=48 * 1024 * 1024
            ),
        )(queries, out_grad, key_states, value_states, doc_lengths)

    return jax.shard_map(
        body,
        mesh=mesh,
        in_specs=(P(("ctx", "kv"), None),) * 4 + (P(),),
        out_specs=(P(("ctx", "kv"), None),) * 4,
        check_vma=False,
    )
```

```python
import functools
import math

import jax
import jax.numpy as jnp
from jax import lax
from jax.experimental import pallas as pl
from jax.experimental.pallas import tpu as pltpu
from jax.sharding import PartitionSpec as P

HEAD_DIM = 128
DOC_MAX = 1024
STEP = 512
MESH = pl.DeviceIdType.MESH


def dot_last(left, right):
    return lax.dot_general(
        left, right, (((1,), (1,)), ((), ())), preferred_element_type=jnp.float32
    )


def dot_plain(left, right):
    return jnp.dot(left, right, preferred_element_type=jnp.float32)


def kernel(
    n_ctx, reach, heads,
    q_hbm, g_hbm, k_hbm, v_hbm, doc_ref,
    att_hbm, dq_hbm, dk_ref, dv_ref,
    qraw, graw, qst, gst, kwin, vwin, kwin_t, vwin_t, bias, exps, gprobs, probs, dscores,
    block_max, block_sum, block_dot, weight, row_dot,
    part_out, part_in, agg_in, agg_out, att_buf, dq_buf,
    load_sem, kv_send, kv_recv, qg_send, qg_recv, relay_send, part_send, part_recv,
    agg_send, agg_recv, out_send, out_recv, out_sem,
):
    c = lax.axis_index("ctx")
    m = lax.axis_index("kv")
    other = 1 - m
    T = k_hbm.shape[0]
    D = HEAD_DIM
    shard = 2 * T
    half_cols = heads * D
    span = reach * shard + T
    factor = 1.0 / math.sqrt(D)

    place = c % reach
    has_next = c + reach < n_ctx
    has_prev = c >= reach

    def sends_to(j):
        return has_next if j == reach else place + j < reach

    def exists(j):
        return c >= j

    barrier = pltpu.get_barrier_semaphore()
    pl.semaphore_signal(barrier, inc=1, device_id=(c, other), device_id_type=MESH)
    for j in range(1, reach):
        for e in range(2):
            near = c - place + (place + j) % reach
            pl.semaphore_signal(barrier, inc=1, device_id=(near, e), device_id_type=MESH)

    @pl.when(has_next)
    def _():
        for e in range(2):
            pl.semaphore_signal(barrier, inc=1, device_id=(c + reach, e), device_id_type=MESH)

    @pl.when(has_prev)
    def _():
        for e in range(2):
            pl.semaphore_signal(barrier, inc=1, device_id=(c - reach, e), device_id_type=MESH)

    own_cols = pl.ds(pl.multiple_of(m * half_cols, D), half_cols)
    own_key_cols = pl.ds(pl.multiple_of(m * D, D), D)
    own_rows = pl.ds(pl.multiple_of(reach * shard + m * T, T), T)
    loads = [
        pltpu.make_async_copy(k_hbm.at[:, own_key_cols], kwin.at[own_rows], load_sem.at[0]),
        pltpu.make_async_copy(v_hbm.at[:, own_key_cols], vwin.at[own_rows], load_sem.at[1]),
        pltpu.make_async_copy(q_hbm.at[:, own_cols], qraw.at[m], load_sem.at[2]),
        pltpu.make_async_copy(g_hbm.at[:, own_cols], graw.at[m], load_sem.at[3]),
    ]
    for copy in loads:
        copy.start()

    peers = 1 + 2 * (reach - 1) + jnp.where(has_next, 2, 0) + jnp.where(has_prev, 2, 0)
    pl.semaphore_wait(barrier, peers)

    def kv_copy(j, dest, sender):
        cols = pl.ds(pl.multiple_of(dest * D, D), D)
        rows = pl.ds(pl.multiple_of((reach - j) * shard + sender * T, T), T)
        copies = []
        for which, (src, dst) in enumerate(((k_hbm, kwin), (v_hbm, vwin))):
            copies.append(
                pltpu.make_async_remote_copy(
                    src_ref=src.at[:, cols],
                    dst_ref=dst.at[rows],
                    send_sem=kv_send.at[(j * 2 + dest) * 2 + which],
                    recv_sem=kv_recv.at[(j * 2 + sender) * 2 + which],
                    device_id=(c + j, dest),
                    device_id_type=MESH,
                )
            )
        return copies

    @pl.when(has_next)
    def _():
        for dest in range(2):
            for copy in kv_copy(reach, dest, m):
                copy.start()

    for copy in kv_copy(0, other, m):
        copy.start()

    def qg_copies(sender, dest):
        cols = pl.ds(pl.multiple_of(dest * half_cols, D), half_cols)
        copies = []
        for which, (src, dst) in enumerate(((q_hbm, qraw), (g_hbm, graw))):
            copies.append(
                pltpu.make_async_remote_copy(
                    src_ref=src.at[:, cols],
                    dst_ref=dst.at[sender],
                    send_sem=qg_send.at[which],
                    recv_sem=qg_recv.at[which],
                    device_id=(c, dest),
                    device_id_type=MESH,
                )
            )
        return copies

    for copy in qg_copies(m, other):
        copy.start()
    for j in range(1, reach):
        @pl.when(sends_to(j))
        def _():
            for dest in range(2):
                for copy in kv_copy(j, dest, m):
                    copy.start()

    def relay_copy(back, sender, which):
        win = (kwin, vwin)[which]
        return pltpu.make_async_remote_copy(
            src_ref=win.at[pl.ds(sender * T, T)],
            dst_ref=win.at[pl.ds(back * shard + sender * T, T)],
            send_sem=relay_send.at[(back * 2 + sender) * 2 + which],
            recv_sem=kv_recv.at[((reach - back) * 2 + sender) * 2 + which],
            device_id=(c - back, m),
            device_id_type=MESH,
        )

    for j in range(1, reach + 1):
        @pl.when(jnp.logical_not(exists(j)))
        def _():
            rows = pl.ds((reach - j) * shard, shard)
            kwin[rows, :] = jnp.zeros((shard, D), kwin.dtype)
            vwin[rows, :] = jnp.zeros((shard, D), vwin.dtype)

        @pl.when(jnp.logical_not(sends_to(j)))
        def _():
            part_in[j] = jnp.zeros(part_in.shape[1:], part_in.dtype)

    for back in range(1, reach):
        @pl.when(place < back)
        def _():
            agg_in[back] = jnp.zeros(agg_in.shape[1:], agg_in.dtype)

    for t in range(2):
        row_pos = c * shard + t * T + lax.broadcasted_iota(jnp.int32, (1, T), 1)
        first = jnp.zeros((1, T), jnp.int32)
        end = jnp.int32(0)
        for d in range(doc_ref.shape[0]):
            end = end + doc_ref[d]
            first = jnp.where(end <= row_pos, end, first)
        key_pos = (c - reach) * shard + t * T + lax.broadcasted_iota(jnp.int32, (span, T), 0)
        allowed = (key_pos >= first) & (key_pos <= row_pos)
        bias[t] = jnp.where(allowed, 0.0, -1e30)

    for copy in loads:
        copy.wait()
    for copy in qg_copies(other, m):
        copy.wait_recv()
    for t in range(2):
        for h in range(heads):
            qst[t, h * T : (h + 1) * T, :] = qraw[t, :, h * D : (h + 1) * D]
            gst[t, h * T : (h + 1) * T, :] = graw[t, :, h * D : (h + 1) * D]
    step_cols = min(STEP, heads * T)
    scale2 = factor * math.log2(math.e)

    def rows_of(j, t):
        low = max((reach - j) * shard, t * T)
        high = min((reach - j + 1) * shard, t * T + span)
        return low, high

    def each_step(run):
        def one(i, carry):
            run(pl.ds(pl.multiple_of(i * step_cols, step_cols), step_cols))
            return carry

        lax.fori_loop(0, heads * T // step_cols, one, 0)

    def score_block(j):
        for t in range(2):
            low, high = rows_of(j, t)

            def run(cols):
                local = slice(low - t * T, high - t * T)
                scores = dot_last(kwin[low:high, :], qst[t, cols, :])
                mask_term = jnp.concatenate([bias[t, local, :]] * (step_cols // T), axis=1)
                z = scores * scale2 + mask_term
                highest = jnp.max(z, axis=0, keepdims=True)
                e = jnp.exp2(z - highest)
                gp = dot_last(vwin[low:high, :], gst[t, cols, :])
                exps[t, local, cols] = e
                gprobs[t, local, cols] = gp
                block_max[j, t, :, cols] = highest
                block_sum[j, t, :, cols] = jnp.sum(e, axis=0, keepdims=True)
                block_dot[j, t, :, cols] = jnp.sum(e * gp, axis=0, keepdims=True)

            each_step(run)

    for copy in kv_copy(0, m, other):
        copy.wait_recv()
    score_block(0)

    @pl.when(has_prev)
    def _():
        for sender in range(2):
            for which, copy in enumerate(kv_copy(reach, m, sender)):
                copy.wait_recv()
                for back in range(1, reach):
                    @pl.when(place >= back)
                    def _():
                        relay_copy(back, sender, which).start()

    score_block(reach)
    for j in range(1, reach):
        @pl.when(exists(j))
        def _():
            for sender in range(2):
                for copy in kv_copy(j, m, sender):
                    copy.wait_recv()

        score_block(j)

    for t in range(2):
        highest = block_max[0, t]
        for j in range(1, reach + 1):
            highest = jnp.maximum(highest, block_max[j, t])
        shrink = [jnp.exp2(block_max[j, t] - highest) for j in range(reach + 1)]
        total = sum(block_sum[j, t] * shrink[j] for j in range(reach + 1))
        inverse = 1.0 / total
        shrink = [value * inverse for value in shrink]
        row_dot[t] = sum(block_dot[j, t] * shrink[j] for j in range(reach + 1))
        for j in range(reach + 1):
            weight[j, t] = shrink[j]

    def part_copy(j, dest, sender):
        return pltpu.make_async_remote_copy(
            src_ref=part_out.at[j, dest],
            dst_ref=part_in.at[j, sender],
            send_sem=part_send.at[j * 2 + dest],
            recv_sem=part_recv.at[j * 2 + sender],
            device_id=(c - j, dest),
            device_id_type=MESH,
        )

    def agg_copy(back):
        return pltpu.make_async_remote_copy(
            src_ref=part_out.at[reach - back],
            dst_ref=agg_in.at[back],
            send_sem=agg_send.at[back],
            recv_sem=agg_recv.at[back],
            device_id=(c + back, m),
            device_id_type=MESH,
        )

    def agg_out_copy(dest, sender):
        return pltpu.make_async_remote_copy(
            src_ref=agg_out.at[dest],
            dst_ref=part_in.at[reach, sender],
            send_sem=part_send.at[reach * 2 + dest],
            recv_sem=part_recv.at[reach * 2 + sender],
            device_id=(c - reach, dest),
            device_id_type=MESH,
        )

    for j in range(reach, -1, -1):
        for t in range(2):
            low, high = rows_of(j, t)

            def run(cols):
                local = slice(low - t * T, high - t * T)
                p = exps[t, local, cols] * weight[j, t, :, cols]
                probs[t, local, cols] = p.astype(jnp.bfloat16)
                ds = p * (gprobs[t, local, cols] - row_dot[t, :, cols])
                dscores[t, local, cols] = ds.astype(jnp.bfloat16)

            each_step(run)
        for which, (lhs, rhs, scale) in enumerate(((dscores, qst, factor), (probs, gst, 1.0))):
            value = []
            for t in range(2):
                low, high = rows_of(j, t)
                value.append(dot_plain(lhs[t, low - t * T : high - t * T, :], rhs[t]) * scale)
            low, high = value
            if j == 0:
                halves = (low + high[:T], high[T:])
            elif j == reach:
                halves = (low[:T], low[T:] + high)
            else:
                halves = (low[:T] + high[:T], low[T:] + high[T:])
            for half in range(2):
                part_out[j, half, which] = halves[half].astype(part_out.dtype)
        if j == 0:
            part_copy(0, other, m).start()
        elif j < reach:
            @pl.when(place >= j)
            def _():
                for dest in range(2):
                    part_copy(j, dest, m).start()

            @pl.when((place < j) & has_prev)
            def _():
                agg_copy(reach - j).start()

    kwin_t[...] = kwin[...].T
    vwin_t[...] = vwin[...].T
    pair = 2 * T

    def remote_out(sender, dest):
        cols = pl.ds(pl.multiple_of(sender * half_cols, D), half_cols)
        return [
            pltpu.make_async_remote_copy(
                src_ref=src.at[dest],
                dst_ref=dst.at[:, cols],
                send_sem=out_send.at[which],
                recv_sem=out_recv.at[which],
                device_id=(c, dest),
                device_id_type=MESH,
            )
            for which, (src, dst) in enumerate(((att_buf, att_hbm), (dq_buf, dq_hbm)))
        ]

    def outputs(t):
        keys = pl.ds(pl.multiple_of(t * T, T), span)

        def one_pair(i, carry):
            cols = pl.ds(pl.multiple_of(i * pair, pair), pair)
            o = dot_plain(vwin_t[:, keys], probs[t, :, cols]).T
            dq = (dot_plain(kwin_t[:, keys], dscores[t, :, cols]) * factor).T
            for a in range(2):
                at = pl.ds(pl.multiple_of(i * 2 * D + a * D, D), D)
                att_buf[t, :, at] = o[a * T : (a + 1) * T].astype(att_buf.dtype)
                dq_buf[t, :, at] = dq[a * T : (a + 1) * T].astype(dq_buf.dtype)
            return carry

        lax.fori_loop(0, heads // 2, one_pair, 0)

    outputs(other)
    for copy in remote_out(m, other):
        copy.start()

    @pl.when(has_prev)
    def _():
        for back in range(1, reach):
            @pl.when(place >= back)
            def _():
                agg_copy(back).wait_recv()

        for dest in range(2):
            for which in range(2):
                total = part_out[reach, dest, which].astype(jnp.float32)
                for back in range(1, reach):
                    total = total + agg_in[back, dest, which].astype(jnp.float32)
                agg_out[dest, which] = total.astype(agg_out.dtype)
            agg_out_copy(dest, m).start()

    outputs(m)
    stores = [
        pltpu.make_async_copy(att_buf.at[m], att_hbm.at[:, own_cols], out_sem.at[0]),
        pltpu.make_async_copy(dq_buf.at[m], dq_hbm.at[:, own_cols], out_sem.at[1]),
    ]
    for copy in stores:
        copy.start()

    part_in[0, m] = part_out[0, m]
    part_copy(0, m, other).wait_recv()
    for j in range(1, reach):
        @pl.when(sends_to(j))
        def _():
            for sender in range(2):
                part_copy(j, m, sender).wait_recv()

    @pl.when(has_next)
    def _():
        for sender in range(2):
            agg_out_copy(m, sender).wait_recv()

    for which, ref in enumerate((dk_ref, dv_ref)):
        for e in range(2):
            total = part_in[0, e, which].astype(jnp.float32)
            for j in range(1, reach + 1):
                total = total + part_in[j, e, which].astype(jnp.float32)
            ref[:, e * D : (e + 1) * D] = total.astype(ref.dtype)

    for copy in stores:
        copy.wait()
    for copy in remote_out(other, m):
        copy.wait_recv()
    for copy in remote_out(m, other):
        copy.wait_send()
    for copy in qg_copies(m, other):
        copy.wait_send()
    for copy in kv_copy(0, other, m):
        copy.wait_send()
    part_copy(0, other, m).wait_send()
    for j in range(1, reach + 1):
        @pl.when(sends_to(j))
        def _():
            for dest in range(2):
                for copy in kv_copy(j, dest, m):
                    copy.wait_send()

    for j in range(1, reach):
        @pl.when(place >= j)
        def _():
            for dest in range(2):
                part_copy(j, dest, m).wait_send()

        @pl.when((place < j) & has_prev)
        def _():
            agg_copy(reach - j).wait_send()

        @pl.when((place >= j) & has_prev)
        def _():
            for sender in range(2):
                for which in range(2):
                    relay_copy(j, sender, which).wait_send()

    @pl.when(has_prev)
    def _():
        for dest in range(2):
            agg_out_copy(dest, m).wait_send()


def solution(mesh):
    n_ctx = mesh.shape["ctx"]

    def body(queries, key_states, value_states, out_grad, doc_lengths):
        T, q_cols = queries.shape
        D = HEAD_DIM
        heads = q_cols // D // 2
        shard = 2 * T
        reach = (DOC_MAX - 1) // shard + 1
        window = (reach + 1) * shard
        span = reach * shard + T
        bf16, f32 = jnp.bfloat16, jnp.float32
        hbm = pl.BlockSpec(memory_space=pl.ANY)
        vmem = pl.BlockSpec(memory_space=pltpu.VMEM)
        dma = pltpu.SemaphoreType.DMA
        return pl.pallas_call(
            functools.partial(kernel, n_ctx, reach, heads),
            out_shape=(
                jax.ShapeDtypeStruct(queries.shape, bf16),
                jax.ShapeDtypeStruct(queries.shape, bf16),
                jax.ShapeDtypeStruct(key_states.shape, bf16),
                jax.ShapeDtypeStruct(key_states.shape, bf16),
            ),
            in_specs=[hbm] * 4 + [pl.BlockSpec(memory_space=pltpu.SMEM)],
            out_specs=(hbm, hbm, vmem, vmem),
            scratch_shapes=[
                pltpu.VMEM((2, T, heads * D), bf16),
                pltpu.VMEM((2, T, heads * D), bf16),
                pltpu.VMEM((2, heads * T, D), bf16),
                pltpu.VMEM((2, heads * T, D), bf16),
                pltpu.VMEM((window, D), bf16),
                pltpu.VMEM((window, D), bf16),
                pltpu.VMEM((D, window), bf16),
                pltpu.VMEM((D, window), bf16),
                pltpu.VMEM((2, span, T), f32),
                pltpu.VMEM((2, span, heads * T), f32),
                pltpu.VMEM((2, span, heads * T), f32),
                pltpu.VMEM((2, span, heads * T), bf16),
                pltpu.VMEM((2, span, heads * T), bf16),
                pltpu.VMEM((reach + 1, 2, 1, heads * T), f32),
                pltpu.VMEM((reach + 1, 2, 1, heads * T), f32),
                pltpu.VMEM((reach + 1, 2, 1, heads * T), f32),
                pltpu.VMEM((reach + 1, 2, 1, heads * T), f32),
                pltpu.VMEM((2, 1, heads * T), f32),
                pltpu.VMEM((reach + 1, 2, 2, T, D), bf16),
                pltpu.VMEM((reach + 1, 2, 2, T, D), bf16),
                pltpu.VMEM((reach, 2, 2, T, D), bf16),
                pltpu.VMEM((2, 2, T, D), bf16),
                pltpu.VMEM((2, T, heads * D), bf16),
                pltpu.VMEM((2, T, heads * D), bf16),
                dma((4,)),
                dma(((reach + 1) * 4,)),
                dma(((reach + 1) * 4,)),
                dma((2,)),
                dma((2,)),
                dma((reach * 4,)),
                dma(((reach + 1) * 2,)),
                dma(((reach + 1) * 2,)),
                dma((reach,)),
                dma((reach,)),
                dma((2,)),
                dma((2,)),
                dma((2,)),
            ],
            compiler_params=pltpu.CompilerParams(
                collective_id=0, has_side_effects=True, vmem_limit_bytes=60 * 1024 * 1024
            ),
        )(queries, out_grad, key_states, value_states, doc_lengths)

    return jax.shard_map(
        body,
        mesh=mesh,
        in_specs=(P(("ctx", "kv"), None),) * 4 + (P(),),
        out_specs=(P(("ctx", "kv"), None),) * 4,
        check_vma=False,
    )
```

```python
import functools
import math

import jax
import jax.numpy as jnp
from jax import lax
from jax.experimental import pallas as pl
from jax.experimental.pallas import tpu as pltpu
from jax.sharding import PartitionSpec as P

HEAD_DIM = 128
DOC_MAX = 1024
STEP = 1024
VMEM_LIMIT = 60 * 1024 * 1024
MESH = pl.DeviceIdType.MESH


def dot_last(left, right):
    return lax.dot_general(
        left, right, (((1,), (1,)), ((), ())), preferred_element_type=jnp.float32
    )


def dot_plain(left, right):
    return jnp.dot(left, right, preferred_element_type=jnp.float32)


def kernel(
    n_ctx, reach, heads,
    q_hbm, g_hbm, k_hbm, v_hbm, doc_ref,
    att_hbm, dq_hbm, dk_ref, dv_ref,
    qraw, graw, qst, gst, kwin, vwin, kwin_t, vwin_t, bias, exps, gprobs, probs, dscores,
    block_max, block_sum, block_dot, weight, row_dot,
    part_out, part_in, agg_in, agg_out, att_buf, dq_buf,
    load_sem, kv_send, kv_recv, qg_send, qg_recv, relay_send, part_send, part_recv,
    agg_send, agg_recv, out_send, out_recv, out_sem,
):
    c = lax.axis_index("ctx")
    m = lax.axis_index("kv")
    other = 1 - m
    T = k_hbm.shape[0]
    D = HEAD_DIM
    shard = 2 * T
    half_cols = heads * D
    span = reach * shard + T
    factor = 1.0 / math.sqrt(D)

    place = c % reach
    has_next = c + reach < n_ctx
    has_prev = c >= reach

    def crosses_to(j):
        return has_next & (2 * place + j == 2 * reach - 1)

    def crosses_from(j):
        return has_prev & (2 * place + 1 == j)

    def sends_to(j):
        return has_next if j == reach else (place + j < reach) | crosses_to(j)

    def direct_back(j):
        return (place >= j) | crosses_from(j)

    def relays(back):
        return has_prev & (place >= back) & (2 * place - back != reach - 1)

    def exists(j):
        return c >= j

    barrier = pltpu.get_barrier_semaphore()
    pl.semaphore_signal(barrier, inc=1, device_id=(c, other), device_id_type=MESH)
    for j in range(1, reach):
        for e in range(2):
            near = c - place + (place + j) % reach
            pl.semaphore_signal(barrier, inc=1, device_id=(near, e), device_id_type=MESH)

        @pl.when(crosses_to(j))
        def _():
            for e in range(2):
                pl.semaphore_signal(barrier, inc=1, device_id=(c + j, e), device_id_type=MESH)

        @pl.when(crosses_from(j))
        def _():
            for e in range(2):
                pl.semaphore_signal(barrier, inc=1, device_id=(c - j, e), device_id_type=MESH)

    @pl.when(has_next)
    def _():
        for e in range(2):
            pl.semaphore_signal(barrier, inc=1, device_id=(c + reach, e), device_id_type=MESH)

    @pl.when(has_prev)
    def _():
        for e in range(2):
            pl.semaphore_signal(barrier, inc=1, device_id=(c - reach, e), device_id_type=MESH)

    own_cols = pl.ds(pl.multiple_of(m * half_cols, D), half_cols)
    own_key_cols = pl.ds(pl.multiple_of(m * D, D), D)
    own_rows = pl.ds(pl.multiple_of(reach * shard + m * T, T), T)
    loads = [
        pltpu.make_async_copy(k_hbm.at[:, own_key_cols], kwin.at[own_rows], load_sem.at[0]),
        pltpu.make_async_copy(v_hbm.at[:, own_key_cols], vwin.at[own_rows], load_sem.at[1]),
        pltpu.make_async_copy(q_hbm.at[:, own_cols], qraw.at[m], load_sem.at[2]),
        pltpu.make_async_copy(g_hbm.at[:, own_cols], graw.at[m], load_sem.at[3]),
    ]
    for copy in loads:
        copy.start()

    peers = 1 + 2 * (reach - 1) + jnp.where(has_next, 2, 0) + jnp.where(has_prev, 2, 0)
    for j in range(1, reach):
        peers = peers + jnp.where(crosses_to(j), 2, 0) + jnp.where(crosses_from(j), 2, 0)
    pl.semaphore_wait(barrier, peers)

    def kv_copy(j, dest, sender):
        cols = pl.ds(pl.multiple_of(dest * D, D), D)
        rows = pl.ds(pl.multiple_of((reach - j) * shard + sender * T, T), T)
        copies = []
        for which, (src, dst) in enumerate(((k_hbm, kwin), (v_hbm, vwin))):
            copies.append(
                pltpu.make_async_remote_copy(
                    src_ref=src.at[:, cols],
                    dst_ref=dst.at[rows],
                    send_sem=kv_send.at[(j * 2 + dest) * 2 + which],
                    recv_sem=kv_recv.at[(j * 2 + sender) * 2 + which],
                    device_id=(c + j, dest),
                    device_id_type=MESH,
                )
            )
        return copies

    @pl.when(has_next)
    def _():
        for dest in range(2):
            for copy in kv_copy(reach, dest, m):
                copy.start()

    for copy in kv_copy(0, other, m):
        copy.start()

    def qg_copies(sender, dest):
        cols = pl.ds(pl.multiple_of(dest * half_cols, D), half_cols)
        copies = []
        for which, (src, dst) in enumerate(((q_hbm, qraw), (g_hbm, graw))):
            copies.append(
                pltpu.make_async_remote_copy(
                    src_ref=src.at[:, cols],
                    dst_ref=dst.at[sender],
                    send_sem=qg_send.at[which],
                    recv_sem=qg_recv.at[which],
                    device_id=(c, dest),
                    device_id_type=MESH,
                )
            )
        return copies

    for copy in qg_copies(m, other):
        copy.start()
    for j in range(1, reach):
        @pl.when(sends_to(j))
        def _():
            for dest in range(2):
                for copy in kv_copy(j, dest, m):
                    copy.start()

    def relay_copy(back, sender, which):
        win = (kwin, vwin)[which]
        return pltpu.make_async_remote_copy(
            src_ref=win.at[pl.ds(sender * T, T)],
            dst_ref=win.at[pl.ds(back * shard + sender * T, T)],
            send_sem=relay_send.at[(back * 2 + sender) * 2 + which],
            recv_sem=kv_recv.at[((reach - back) * 2 + sender) * 2 + which],
            device_id=(c - back, m),
            device_id_type=MESH,
        )

    for j in range(1, reach + 1):
        @pl.when(jnp.logical_not(exists(j)))
        def _():
            rows = pl.ds((reach - j) * shard, shard)
            kwin[rows, :] = jnp.zeros((shard, D), kwin.dtype)
            vwin[rows, :] = jnp.zeros((shard, D), vwin.dtype)

        @pl.when(jnp.logical_not(sends_to(j)))
        def _():
            part_in[j] = jnp.zeros(part_in.shape[1:], part_in.dtype)

    for back in range(1, reach):
        @pl.when(jnp.logical_not(relays(back)))
        def _():
            agg_in[back] = jnp.zeros(agg_in.shape[1:], agg_in.dtype)

    for t in range(2):
        row_pos = c * shard + t * T + lax.broadcasted_iota(jnp.int32, (1, T), 1)
        first = jnp.zeros((1, T), jnp.int32)
        end = jnp.int32(0)
        for d in range(doc_ref.shape[0]):
            end = end + doc_ref[d]
            first = jnp.where(end <= row_pos, end, first)
        key_pos = (c - reach) * shard + t * T + lax.broadcasted_iota(jnp.int32, (span, T), 0)
        allowed = (key_pos >= first) & (key_pos <= row_pos)
        bias[t] = jnp.where(allowed, 0.0, -1e30)

    @pl.when(has_prev)
    def _():
        for sender in range(2):
            for which, copy in enumerate(kv_copy(reach, m, sender)):
                copy.wait_recv()
                for back in range(1, reach):
                    @pl.when(relays(back))
                    def _():
                        relay_copy(back, sender, which).start()

    for copy in loads:
        copy.wait()
    for copy in qg_copies(other, m):
        copy.wait_recv()
    for t in range(2):
        for h in range(heads):
            qst[t, h * T : (h + 1) * T, :] = qraw[t, :, h * D : (h + 1) * D]
            gst[t, h * T : (h + 1) * T, :] = graw[t, :, h * D : (h + 1) * D]
    step_cols = min(STEP, heads * T)
    scale2 = factor * math.log2(math.e)

    def rows_of(j, t):
        low = max((reach - j) * shard, t * T)
        high = min((reach - j + 1) * shard, t * T + span)
        return low, high

    def each_step(run):
        def one(i, carry):
            run(pl.ds(pl.multiple_of(i * step_cols, step_cols), step_cols))
            return carry

        lax.fori_loop(0, heads * T // step_cols, one, 0)

    def score_block(j):
        for t in range(2):
            low, high = rows_of(j, t)

            def run(cols):
                local = slice(low - t * T, high - t * T)
                scores = dot_last(kwin[low:high, :], qst[t, cols, :])
                mask_term = jnp.concatenate([bias[t, local, :]] * (step_cols // T), axis=1)
                z = scores * scale2 + mask_term
                highest = jnp.max(z, axis=0, keepdims=True)
                e = jnp.exp2(z - highest)
                gp = dot_last(vwin[low:high, :], gst[t, cols, :])
                exps[t, local, cols] = e
                gprobs[t, local, cols] = gp
                block_max[j, t, :, cols] = highest
                block_sum[j, t, :, cols] = jnp.sum(e, axis=0, keepdims=True)
                block_dot[j, t, :, cols] = jnp.sum(e * gp, axis=0, keepdims=True)

            each_step(run)

    for copy in kv_copy(0, m, other):
        copy.wait_recv()
    score_block(0)

    score_block(reach)
    for j in range(1, reach):
        @pl.when(exists(j))
        def _():
            for sender in range(2):
                for copy in kv_copy(j, m, sender):
                    copy.wait_recv()

        score_block(j)

    for t in range(2):
        highest = block_max[0, t]
        for j in range(1, reach + 1):
            highest = jnp.maximum(highest, block_max[j, t])
        shrink = [jnp.exp2(block_max[j, t] - highest) for j in range(reach + 1)]
        total = sum(block_sum[j, t] * shrink[j] for j in range(reach + 1))
        inverse = 1.0 / total
        shrink = [value * inverse for value in shrink]
        row_dot[t] = sum(block_dot[j, t] * shrink[j] for j in range(reach + 1))
        for j in range(reach + 1):
            weight[j, t] = shrink[j]

    def part_copy(j, dest, sender):
        return pltpu.make_async_remote_copy(
            src_ref=part_out.at[j, dest],
            dst_ref=part_in.at[j, sender],
            send_sem=part_send.at[j * 2 + dest],
            recv_sem=part_recv.at[j * 2 + sender],
            device_id=(c - j, dest),
            device_id_type=MESH,
        )

    def agg_copy(back):
        return pltpu.make_async_remote_copy(
            src_ref=part_out.at[reach - back],
            dst_ref=agg_in.at[back],
            send_sem=agg_send.at[back],
            recv_sem=agg_recv.at[back],
            device_id=(c + back, m),
            device_id_type=MESH,
        )

    def agg_out_copy(dest, sender):
        return pltpu.make_async_remote_copy(
            src_ref=agg_out.at[dest],
            dst_ref=part_in.at[reach, sender],
            send_sem=part_send.at[reach * 2 + dest],
            recv_sem=part_recv.at[reach * 2 + sender],
            device_id=(c - reach, dest),
            device_id_type=MESH,
        )

    for j in (*range(reach - 1, 0, -1), reach, 0):
        for t in range(2):
            low, high = rows_of(j, t)

            def run(cols):
                local = slice(low - t * T, high - t * T)
                p = exps[t, local, cols] * weight[j, t, :, cols]
                probs[t, local, cols] = p.astype(jnp.bfloat16)
                ds = p * (gprobs[t, local, cols] - row_dot[t, :, cols])
                dscores[t, local, cols] = ds.astype(jnp.bfloat16)

            each_step(run)
        for which, (lhs, rhs, scale) in enumerate(((dscores, qst, factor), (probs, gst, 1.0))):
            value = []
            for t in range(2):
                low, high = rows_of(j, t)
                value.append(dot_plain(lhs[t, low - t * T : high - t * T, :], rhs[t]) * scale)
            low, high = value
            if j == 0:
                halves = (low + high[:T], high[T:])
            elif j == reach:
                halves = (low[:T], low[T:] + high)
            else:
                halves = (low[:T] + high[:T], low[T:] + high[T:])
            for half in range(2):
                part_out[j, half, which] = halves[half].astype(part_out.dtype)
        if j == 0:
            part_copy(0, other, m).start()
        elif j < reach:
            @pl.when(direct_back(j))
            def _():
                for dest in range(2):
                    part_copy(j, dest, m).start()

            @pl.when((place < j) & has_prev & (2 * place + 1 != j))
            def _():
                agg_copy(reach - j).start()

    kwin_t[...] = kwin[...].T
    vwin_t[...] = vwin[...].T
    out_heads = min(4, heads)
    pair = out_heads * T

    def remote_out(sender, dest):
        cols = pl.ds(pl.multiple_of(sender * half_cols, D), half_cols)
        return [
            pltpu.make_async_remote_copy(
                src_ref=src.at[dest],
                dst_ref=dst.at[:, cols],
                send_sem=out_send.at[which],
                recv_sem=out_recv.at[which],
                device_id=(c, dest),
                device_id_type=MESH,
            )
            for which, (src, dst) in enumerate(((att_buf, att_hbm), (dq_buf, dq_hbm)))
        ]

    def outputs(t):
        keys = pl.ds(pl.multiple_of(t * T, T), span)

        def one_pair(i, carry):
            cols = pl.ds(pl.multiple_of(i * pair, pair), pair)
            o = dot_plain(vwin_t[:, keys], probs[t, :, cols]).T
            dq = (dot_plain(kwin_t[:, keys], dscores[t, :, cols]) * factor).T
            for a in range(out_heads):
                at = pl.ds(pl.multiple_of(i * pair + a * D, D), D)
                att_buf[t, :, at] = o[a * T : (a + 1) * T].astype(att_buf.dtype)
                dq_buf[t, :, at] = dq[a * T : (a + 1) * T].astype(dq_buf.dtype)
            return carry

        lax.fori_loop(0, heads // out_heads, one_pair, 0)

    outputs(other)
    for copy in remote_out(m, other):
        copy.start()

    @pl.when(has_prev)
    def _():
        for back in range(1, reach):
            @pl.when(relays(back))
            def _():
                agg_copy(back).wait_recv()

        for dest in range(2):
            for which in range(2):
                total = part_out[reach, dest, which].astype(jnp.float32)
                for back in range(1, reach):
                    total = total + agg_in[back, dest, which].astype(jnp.float32)
                agg_out[dest, which] = total.astype(agg_out.dtype)
            agg_out_copy(dest, m).start()

    outputs(m)
    stores = [
        pltpu.make_async_copy(att_buf.at[m], att_hbm.at[:, own_cols], out_sem.at[0]),
        pltpu.make_async_copy(dq_buf.at[m], dq_hbm.at[:, own_cols], out_sem.at[1]),
    ]
    for copy in stores:
        copy.start()

    part_in[0, m] = part_out[0, m]
    part_copy(0, m, other).wait_recv()
    for j in range(1, reach):
        @pl.when(sends_to(j))
        def _():
            for sender in range(2):
                part_copy(j, m, sender).wait_recv()

    @pl.when(has_next)
    def _():
        for sender in range(2):
            agg_out_copy(m, sender).wait_recv()

    for which, ref in enumerate((dk_ref, dv_ref)):
        for e in range(2):
            total = part_in[0, e, which].astype(jnp.float32)
            for j in range(1, reach + 1):
                total = total + part_in[j, e, which].astype(jnp.float32)
            ref[:, e * D : (e + 1) * D] = total.astype(ref.dtype)

    for copy in stores:
        copy.wait()
    for copy in remote_out(other, m):
        copy.wait_recv()
    for copy in remote_out(m, other):
        copy.wait_send()
    for copy in qg_copies(m, other):
        copy.wait_send()
    for copy in kv_copy(0, other, m):
        copy.wait_send()
    part_copy(0, other, m).wait_send()
    for j in range(1, reach + 1):
        @pl.when(sends_to(j))
        def _():
            for dest in range(2):
                for copy in kv_copy(j, dest, m):
                    copy.wait_send()

    for j in range(1, reach):
        @pl.when(direct_back(j))
        def _():
            for dest in range(2):
                part_copy(j, dest, m).wait_send()

        @pl.when((place < j) & has_prev & (2 * place + 1 != j))
        def _():
            agg_copy(reach - j).wait_send()

        @pl.when(relays(j))
        def _():
            for sender in range(2):
                for which in range(2):
                    relay_copy(j, sender, which).wait_send()

    @pl.when(has_prev)
    def _():
        for dest in range(2):
            agg_out_copy(dest, m).wait_send()


def place_results(*refs):
    sources, results, held = refs[:4], refs[4:8], refs[8:12]
    in_sem, out_sem = refs[12:]
    fetches = [pltpu.make_async_copy(sources[i], held[i], in_sem.at[i]) for i in range(4)]
    stores = [pltpu.make_async_copy(held[i], results[i], out_sem.at[i]) for i in range(4)]
    for copy in fetches:
        copy.start()
    for i in range(4):
        fetches[i].wait()
        stores[i].start()
    for copy in stores:
        copy.wait()


def solution(mesh):
    n_ctx = mesh.shape["ctx"]

    def body(queries, key_states, value_states, out_grad, doc_lengths):
        T, q_cols = queries.shape
        D = HEAD_DIM
        heads = q_cols // D // 2
        shard = 2 * T
        reach = (DOC_MAX - 1) // shard + 1
        window = (reach + 1) * shard
        span = reach * shard + T
        bf16, f32 = jnp.bfloat16, jnp.float32
        hbm = pl.BlockSpec(memory_space=pl.ANY)
        vmem = pl.BlockSpec(memory_space=pltpu.VMEM)
        dma = pltpu.SemaphoreType.DMA
        results = pl.pallas_call(
            functools.partial(kernel, n_ctx, reach, heads),
            out_shape=(
                jax.ShapeDtypeStruct(queries.shape, bf16),
                jax.ShapeDtypeStruct(queries.shape, bf16),
                jax.ShapeDtypeStruct(key_states.shape, bf16),
                jax.ShapeDtypeStruct(key_states.shape, bf16),
            ),
            in_specs=[hbm] * 4 + [pl.BlockSpec(memory_space=pltpu.SMEM)],
            out_specs=(hbm, hbm, vmem, vmem),
            scratch_shapes=[
                pltpu.VMEM((2, T, heads * D), bf16),
                pltpu.VMEM((2, T, heads * D), bf16),
                pltpu.VMEM((2, heads * T, D), bf16),
                pltpu.VMEM((2, heads * T, D), bf16),
                pltpu.VMEM((window, D), bf16),
                pltpu.VMEM((window, D), bf16),
                pltpu.VMEM((D, window), bf16),
                pltpu.VMEM((D, window), bf16),
                pltpu.VMEM((2, span, T), f32),
                pltpu.VMEM((2, span, heads * T), f32),
                pltpu.VMEM((2, span, heads * T), f32),
                pltpu.VMEM((2, span, heads * T), bf16),
                pltpu.VMEM((2, span, heads * T), bf16),
                pltpu.VMEM((reach + 1, 2, 1, heads * T), f32),
                pltpu.VMEM((reach + 1, 2, 1, heads * T), f32),
                pltpu.VMEM((reach + 1, 2, 1, heads * T), f32),
                pltpu.VMEM((reach + 1, 2, 1, heads * T), f32),
                pltpu.VMEM((2, 1, heads * T), f32),
                pltpu.VMEM((reach + 1, 2, 2, T, D), bf16),
                pltpu.VMEM((reach + 1, 2, 2, T, D), bf16),
                pltpu.VMEM((reach, 2, 2, T, D), bf16),
                pltpu.VMEM((2, 2, T, D), bf16),
                pltpu.VMEM((2, T, heads * D), bf16),
                pltpu.VMEM((2, T, heads * D), bf16),
                dma((4,)),
                dma(((reach + 1) * 4,)),
                dma(((reach + 1) * 4,)),
                dma((2,)),
                dma((2,)),
                dma((reach * 4,)),
                dma(((reach + 1) * 2,)),
                dma(((reach + 1) * 2,)),
                dma((reach,)),
                dma((reach,)),
                dma((2,)),
                dma((2,)),
                dma((2,)),
            ],
            compiler_params=pltpu.CompilerParams(
                collective_id=0, has_side_effects=True, vmem_limit_bytes=VMEM_LIMIT
            ),
        )(queries, out_grad, key_states, value_states, doc_lengths)
        return pl.pallas_call(
            place_results,
            out_shape=tuple(jax.ShapeDtypeStruct(x.shape, x.dtype) for x in results),
            in_specs=[hbm] * 4,
            out_specs=(hbm,) * 4,
            scratch_shapes=[pltpu.VMEM(x.shape, x.dtype) for x in results] + [dma((4,)), dma((4,))],
            compiler_params=pltpu.CompilerParams(vmem_limit_bytes=VMEM_LIMIT),
        )(*results)

    return jax.shard_map(
        body,
        mesh=mesh,
        in_specs=(P(("ctx", "kv"), None),) * 4 + (P(),),
        out_specs=(P(("ctx", "kv"), None),) * 4,
        check_vma=False,
    )
```

```python
import functools
import math

import jax
import jax.numpy as jnp
from jax import lax
from jax.experimental import pallas as pl
from jax.experimental.pallas import tpu as pltpu
from jax.sharding import PartitionSpec as P

HEAD_DIM = 128
DOC_MAX = 1024
STEP = 1024
VMEM_LIMIT = 60 * 1024 * 1024
MESH = pl.DeviceIdType.MESH


def dot_last(left, right):
    return lax.dot_general(
        left, right, (((1,), (1,)), ((), ())), preferred_element_type=jnp.float32
    )


def dot_plain(left, right):
    return jnp.dot(left, right, preferred_element_type=jnp.float32)


def kernel(
    n_ctx, reach, heads,
    q_hbm, g_hbm, k_hbm, v_hbm, doc_ref,
    att_hbm, dq_hbm, dk_ref, dv_ref,
    qraw, graw, qst, gst, kwin, vwin, kwin_t, vwin_t, bias, exps, gprobs, probs, dscores,
    block_max, block_sum, block_dot, weight, row_dot,
    part_out, part_in, agg_in, agg_out, att_buf, dq_buf,
    load_sem, kv_send, kv_recv, qg_send, qg_recv, relay_send, part_send, part_recv,
    agg_send, agg_recv, out_send, out_recv, out_sem,
):
    c = lax.axis_index("ctx")
    m = lax.axis_index("kv")
    other = 1 - m
    T = k_hbm.shape[0]
    D = HEAD_DIM
    shard = 2 * T
    half_cols = heads * D
    span = reach * shard + T
    factor = 1.0 / math.sqrt(D)

    place = c % reach
    has_next = c + reach < n_ctx
    has_prev = c >= reach

    def crosses_to(j):
        return has_next & (2 * place + j == 2 * reach - 1)

    def crosses_from(j):
        return has_prev & (2 * place + 1 == j)

    def sends_to(j):
        return has_next if j == reach else (place + j < reach) | crosses_to(j)

    def direct_back(j):
        return (place >= j) | crosses_from(j)

    def relays(back):
        return has_prev & (place >= back) & (2 * place - back != reach - 1)

    def exists(j):
        return c >= j

    barrier = pltpu.get_barrier_semaphore()
    pl.semaphore_signal(barrier, inc=1, device_id=(c, other), device_id_type=MESH)
    for j in range(1, reach):
        for e in range(2):
            near = c - place + (place + j) % reach
            pl.semaphore_signal(barrier, inc=1, device_id=(near, e), device_id_type=MESH)

        @pl.when(crosses_to(j))
        def _():
            for e in range(2):
                pl.semaphore_signal(barrier, inc=1, device_id=(c + j, e), device_id_type=MESH)

        @pl.when(crosses_from(j))
        def _():
            for e in range(2):
                pl.semaphore_signal(barrier, inc=1, device_id=(c - j, e), device_id_type=MESH)

    @pl.when(has_next)
    def _():
        for e in range(2):
            pl.semaphore_signal(barrier, inc=1, device_id=(c + reach, e), device_id_type=MESH)

    @pl.when(has_prev)
    def _():
        for e in range(2):
            pl.semaphore_signal(barrier, inc=1, device_id=(c - reach, e), device_id_type=MESH)

    own_cols = pl.ds(pl.multiple_of(m * half_cols, D), half_cols)
    own_key_cols = pl.ds(pl.multiple_of(m * D, D), D)
    own_rows = pl.ds(pl.multiple_of(reach * shard + m * T, T), T)
    loads = [
        pltpu.make_async_copy(k_hbm.at[:, own_key_cols], kwin.at[own_rows], load_sem.at[0]),
        pltpu.make_async_copy(v_hbm.at[:, own_key_cols], vwin.at[own_rows], load_sem.at[1]),
        pltpu.make_async_copy(q_hbm.at[:, own_cols], qraw.at[m], load_sem.at[2]),
        pltpu.make_async_copy(g_hbm.at[:, own_cols], graw.at[m], load_sem.at[3]),
    ]
    for copy in loads:
        copy.start()

    peers = 1 + 2 * (reach - 1) + jnp.where(has_next, 2, 0) + jnp.where(has_prev, 2, 0)
    for j in range(1, reach):
        peers = peers + jnp.where(crosses_to(j), 2, 0) + jnp.where(crosses_from(j), 2, 0)
    pl.semaphore_wait(barrier, peers)

    def kv_copy(j, dest, sender):
        cols = pl.ds(pl.multiple_of(dest * D, D), D)
        rows = pl.ds(pl.multiple_of((reach - j) * shard + sender * T, T), T)
        copies = []
        for which, (src, dst) in enumerate(((k_hbm, kwin), (v_hbm, vwin))):
            copies.append(
                pltpu.make_async_remote_copy(
                    src_ref=src.at[:, cols],
                    dst_ref=dst.at[rows],
                    send_sem=kv_send.at[(j * 2 + dest) * 2 + which],
                    recv_sem=kv_recv.at[(j * 2 + sender) * 2 + which],
                    device_id=(c + j, dest),
                    device_id_type=MESH,
                )
            )
        return copies

    @pl.when(has_next)
    def _():
        for dest in range(2):
            for copy in kv_copy(reach, dest, m):
                copy.start()

    for copy in kv_copy(0, other, m):
        copy.start()

    def qg_copies(sender, dest):
        cols = pl.ds(pl.multiple_of(dest * half_cols, D), half_cols)
        copies = []
        for which, (src, dst) in enumerate(((q_hbm, qraw), (g_hbm, graw))):
            copies.append(
                pltpu.make_async_remote_copy(
                    src_ref=src.at[:, cols],
                    dst_ref=dst.at[sender],
                    send_sem=qg_send.at[which],
                    recv_sem=qg_recv.at[which],
                    device_id=(c, dest),
                    device_id_type=MESH,
                )
            )
        return copies

    for copy in qg_copies(m, other):
        copy.start()
    for j in range(1, reach):
        @pl.when(sends_to(j))
        def _():
            for dest in range(2):
                for copy in kv_copy(j, dest, m):
                    copy.start()

    def relay_copy(back, sender, which):
        win = (kwin, vwin)[which]
        return pltpu.make_async_remote_copy(
            src_ref=win.at[pl.ds(sender * T, T)],
            dst_ref=win.at[pl.ds(back * shard + sender * T, T)],
            send_sem=relay_send.at[(back * 2 + sender) * 2 + which],
            recv_sem=kv_recv.at[((reach - back) * 2 + sender) * 2 + which],
            device_id=(c - back, m),
            device_id_type=MESH,
        )

    for j in range(1, reach + 1):
        @pl.when(jnp.logical_not(exists(j)))
        def _():
            rows = pl.ds((reach - j) * shard, shard)
            kwin[rows, :] = jnp.zeros((shard, D), kwin.dtype)
            vwin[rows, :] = jnp.zeros((shard, D), vwin.dtype)

        @pl.when(jnp.logical_not(sends_to(j)))
        def _():
            part_in[j] = jnp.zeros(part_in.shape[1:], part_in.dtype)

    for back in range(1, reach):
        @pl.when(jnp.logical_not(relays(back)))
        def _():
            agg_in[back] = jnp.zeros(agg_in.shape[1:], agg_in.dtype)

    for t in range(2):
        row_pos = c * shard + t * T + lax.broadcasted_iota(jnp.int32, (1, T), 1)
        first = jnp.zeros((1, T), jnp.int32)
        end = jnp.int32(0)
        for d in range(doc_ref.shape[0]):
            end = end + doc_ref[d]
            first = jnp.where(end <= row_pos, end, first)
        key_pos = (c - reach) * shard + t * T + lax.broadcasted_iota(jnp.int32, (span, T), 0)
        allowed = (key_pos >= first) & (key_pos <= row_pos)
        bias[t] = jnp.where(allowed, 0.0, -1e30)

    @pl.when(has_prev)
    def _():
        for sender in range(2):
            for which, copy in enumerate(kv_copy(reach, m, sender)):
                copy.wait_recv()
                for back in range(1, reach):
                    @pl.when(relays(back))
                    def _():
                        relay_copy(back, sender, which).start()

    for copy in loads:
        copy.wait()
    for copy in qg_copies(other, m):
        copy.wait_recv()
    for t in range(2):
        for h in range(heads):
            qst[t, h * T : (h + 1) * T, :] = qraw[t, :, h * D : (h + 1) * D]
            gst[t, h * T : (h + 1) * T, :] = graw[t, :, h * D : (h + 1) * D]
    step_cols = min(STEP, heads * T)
    scale2 = factor * math.log2(math.e)

    def rows_of(j, t):
        low = max((reach - j) * shard, t * T)
        high = min((reach - j + 1) * shard, t * T + span)
        return low, high

    def each_step(run):
        def one(i, carry):
            run(pl.ds(pl.multiple_of(i * step_cols, step_cols), step_cols))
            return carry

        lax.fori_loop(0, heads * T // step_cols, one, 0)

    def score_block(j):
        for t in range(2):
            low, high = rows_of(j, t)

            def run(cols):
                local = slice(low - t * T, high - t * T)
                scores = dot_last(kwin[low:high, :], qst[t, cols, :])
                mask_term = jnp.concatenate([bias[t, local, :]] * (step_cols // T), axis=1)
                z = scores * scale2 + mask_term
                highest = jnp.max(z, axis=0, keepdims=True)
                e = jnp.exp2(z - highest)
                gp = dot_last(vwin[low:high, :], gst[t, cols, :])
                exps[t, local, cols] = e
                gprobs[t, local, cols] = gp
                block_max[j, t, :, cols] = highest
                block_sum[j, t, :, cols] = jnp.sum(e, axis=0, keepdims=True)
                block_dot[j, t, :, cols] = jnp.sum(e * gp, axis=0, keepdims=True)

            each_step(run)

    for copy in kv_copy(0, m, other):
        copy.wait_recv()
    score_block(0)

    score_block(reach)
    for j in range(1, reach):
        @pl.when(exists(j))
        def _():
            for sender in range(2):
                for copy in kv_copy(j, m, sender):
                    copy.wait_recv()

        score_block(j)

    for t in range(2):
        highest = block_max[0, t]
        for j in range(1, reach + 1):
            highest = jnp.maximum(highest, block_max[j, t])
        shrink = [jnp.exp2(block_max[j, t] - highest) for j in range(reach + 1)]
        total = sum(block_sum[j, t] * shrink[j] for j in range(reach + 1))
        inverse = 1.0 / total
        shrink = [value * inverse for value in shrink]
        row_dot[t] = sum(block_dot[j, t] * shrink[j] for j in range(reach + 1))
        for j in range(reach + 1):
            weight[j, t] = shrink[j]

    def part_copy(j, dest, sender):
        return pltpu.make_async_remote_copy(
            src_ref=part_out.at[j, dest],
            dst_ref=part_in.at[j, sender],
            send_sem=part_send.at[j * 2 + dest],
            recv_sem=part_recv.at[j * 2 + sender],
            device_id=(c - j, dest),
            device_id_type=MESH,
        )

    def agg_copy(back, half):
        return pltpu.make_async_remote_copy(
            src_ref=part_out.at[reach - back, half],
            dst_ref=agg_in.at[back, half],
            send_sem=agg_send.at[back * 2 + half],
            recv_sem=agg_recv.at[back * 2 + half],
            device_id=(c + back, m),
            device_id_type=MESH,
        )

    def agg_out_copy(dest, sender):
        return pltpu.make_async_remote_copy(
            src_ref=agg_out.at[dest],
            dst_ref=part_in.at[reach, sender],
            send_sem=part_send.at[reach * 2 + dest],
            recv_sem=part_recv.at[reach * 2 + sender],
            device_id=(c - reach, dest),
            device_id_type=MESH,
        )

    for j in (*range(reach - 1, 0, -1), reach, 0):
        for t in range(2):
            low, high = rows_of(j, t)

            def run(cols):
                local = slice(low - t * T, high - t * T)
                p = exps[t, local, cols] * weight[j, t, :, cols]
                probs[t, local, cols] = p.astype(jnp.bfloat16)
                ds = p * (gprobs[t, local, cols] - row_dot[t, :, cols])
                dscores[t, local, cols] = ds.astype(jnp.bfloat16)

            each_step(run)
        for which, (lhs, rhs, scale) in enumerate(((dscores, qst, factor), (probs, gst, 1.0))):
            value = []
            for t in range(2):
                low, high = rows_of(j, t)
                value.append(dot_plain(lhs[t, low - t * T : high - t * T, :], rhs[t]) * scale)
            low, high = value
            if j == 0:
                halves = (low + high[:T], high[T:])
            elif j == reach:
                halves = (low[:T], low[T:] + high)
            else:
                halves = (low[:T] + high[:T], low[T:] + high[T:])
            for half in range(2):
                part_out[j, half, which] = halves[half].astype(part_out.dtype)
        if j == 0:
            part_copy(0, other, m).start()
        elif j < reach:
            @pl.when(direct_back(j))
            def _():
                for dest in range(2):
                    part_copy(j, dest, m).start()

            @pl.when((place < j) & has_prev & (2 * place + 1 != j))
            def _():
                for half in range(2):
                    agg_copy(reach - j, half).start()

    kwin_t[...] = kwin[...].T
    vwin_t[...] = vwin[...].T
    out_heads = min(4, heads)
    pair = out_heads * T

    def remote_out(sender, dest):
        cols = pl.ds(pl.multiple_of(sender * half_cols, D), half_cols)
        return [
            pltpu.make_async_remote_copy(
                src_ref=src.at[dest],
                dst_ref=dst.at[:, cols],
                send_sem=out_send.at[which],
                recv_sem=out_recv.at[which],
                device_id=(c, dest),
                device_id_type=MESH,
            )
            for which, (src, dst) in enumerate(((att_buf, att_hbm), (dq_buf, dq_hbm)))
        ]

    def outputs(t):
        keys = pl.ds(pl.multiple_of(t * T, T), span)

        def one_pair(i, carry):
            cols = pl.ds(pl.multiple_of(i * pair, pair), pair)
            o = dot_plain(vwin_t[:, keys], probs[t, :, cols]).T
            dq = (dot_plain(kwin_t[:, keys], dscores[t, :, cols]) * factor).T
            for a in range(out_heads):
                at = pl.ds(pl.multiple_of(i * pair + a * D, D), D)
                att_buf[t, :, at] = o[a * T : (a + 1) * T].astype(att_buf.dtype)
                dq_buf[t, :, at] = dq[a * T : (a + 1) * T].astype(dq_buf.dtype)
            return carry

        lax.fori_loop(0, heads // out_heads, one_pair, 0)

    outputs(other)
    for copy in remote_out(m, other):
        copy.start()

    @pl.when(has_prev)
    def _():
        for dest in range(2):
            for back in range(1, reach):
                @pl.when(relays(back))
                def _():
                    agg_copy(back, dest).wait_recv()

            for which in range(2):
                total = part_out[reach, dest, which].astype(jnp.float32)
                for back in range(1, reach):
                    total = total + agg_in[back, dest, which].astype(jnp.float32)
                agg_out[dest, which] = total.astype(agg_out.dtype)
            agg_out_copy(dest, m).start()

    outputs(m)
    stores = [
        pltpu.make_async_copy(att_buf.at[m], att_hbm.at[:, own_cols], out_sem.at[0]),
        pltpu.make_async_copy(dq_buf.at[m], dq_hbm.at[:, own_cols], out_sem.at[1]),
    ]
    for copy in stores:
        copy.start()

    part_in[0, m] = part_out[0, m]
    part_copy(0, m, other).wait_recv()
    for j in range(1, reach):
        @pl.when(sends_to(j))
        def _():
            for sender in range(2):
                part_copy(j, m, sender).wait_recv()

    @pl.when(has_next)
    def _():
        for sender in range(2):
            agg_out_copy(m, sender).wait_recv()

    for which, ref in enumerate((dk_ref, dv_ref)):
        for e in range(2):
            total = part_in[0, e, which].astype(jnp.float32)
            for j in range(1, reach + 1):
                total = total + part_in[j, e, which].astype(jnp.float32)
            ref[:, e * D : (e + 1) * D] = total.astype(ref.dtype)

    for copy in stores:
        copy.wait()
    for copy in remote_out(other, m):
        copy.wait_recv()
    for copy in remote_out(m, other):
        copy.wait_send()
    for copy in qg_copies(m, other):
        copy.wait_send()
    for copy in kv_copy(0, other, m):
        copy.wait_send()
    part_copy(0, other, m).wait_send()
    for j in range(1, reach + 1):
        @pl.when(sends_to(j))
        def _():
            for dest in range(2):
                for copy in kv_copy(j, dest, m):
                    copy.wait_send()

    for j in range(1, reach):
        @pl.when(direct_back(j))
        def _():
            for dest in range(2):
                part_copy(j, dest, m).wait_send()

        @pl.when((place < j) & has_prev & (2 * place + 1 != j))
        def _():
            for half in range(2):
                agg_copy(reach - j, half).wait_send()

        @pl.when(relays(j))
        def _():
            for sender in range(2):
                for which in range(2):
                    relay_copy(j, sender, which).wait_send()

    @pl.when(has_prev)
    def _():
        for dest in range(2):
            agg_out_copy(dest, m).wait_send()


def place_results(*refs):
    sources, results, held = refs[:4], refs[4:8], refs[8:12]
    in_sem, out_sem = refs[12:]
    fetches = [pltpu.make_async_copy(sources[i], held[i], in_sem.at[i]) for i in range(4)]
    stores = [pltpu.make_async_copy(held[i], results[i], out_sem.at[i]) for i in range(4)]
    for copy in fetches:
        copy.start()
    for i in range(4):
        fetches[i].wait()
        stores[i].start()
    for copy in stores:
        copy.wait()


def solution(mesh):
    n_ctx = mesh.shape["ctx"]

    def body(queries, key_states, value_states, out_grad, doc_lengths):
        T, q_cols = queries.shape
        D = HEAD_DIM
        heads = q_cols // D // 2
        shard = 2 * T
        reach = (DOC_MAX - 1) // shard + 1
        window = (reach + 1) * shard
        span = reach * shard + T
        bf16, f32 = jnp.bfloat16, jnp.float32
        hbm = pl.BlockSpec(memory_space=pl.ANY)
        vmem = pl.BlockSpec(memory_space=pltpu.VMEM)
        dma = pltpu.SemaphoreType.DMA
        results = pl.pallas_call(
            functools.partial(kernel, n_ctx, reach, heads),
            out_shape=(
                jax.ShapeDtypeStruct(queries.shape, bf16),
                jax.ShapeDtypeStruct(queries.shape, bf16),
                jax.ShapeDtypeStruct(key_states.shape, bf16),
                jax.ShapeDtypeStruct(key_states.shape, bf16),
            ),
            in_specs=[hbm] * 4 + [pl.BlockSpec(memory_space=pltpu.SMEM)],
            out_specs=(hbm, hbm, vmem, vmem),
            scratch_shapes=[
                pltpu.VMEM((2, T, heads * D), bf16),
                pltpu.VMEM((2, T, heads * D), bf16),
                pltpu.VMEM((2, heads * T, D), bf16),
                pltpu.VMEM((2, heads * T, D), bf16),
                pltpu.VMEM((window, D), bf16),
                pltpu.VMEM((window, D), bf16),
                pltpu.VMEM((D, window), bf16),
                pltpu.VMEM((D, window), bf16),
                pltpu.VMEM((2, span, T), f32),
                pltpu.VMEM((2, span, heads * T), f32),
                pltpu.VMEM((2, span, heads * T), f32),
                pltpu.VMEM((2, span, heads * T), bf16),
                pltpu.VMEM((2, span, heads * T), bf16),
                pltpu.VMEM((reach + 1, 2, 1, heads * T), f32),
                pltpu.VMEM((reach + 1, 2, 1, heads * T), f32),
                pltpu.VMEM((reach + 1, 2, 1, heads * T), f32),
                pltpu.VMEM((reach + 1, 2, 1, heads * T), f32),
                pltpu.VMEM((2, 1, heads * T), f32),
                pltpu.VMEM((reach + 1, 2, 2, T, D), bf16),
                pltpu.VMEM((reach + 1, 2, 2, T, D), bf16),
                pltpu.VMEM((reach, 2, 2, T, D), bf16),
                pltpu.VMEM((2, 2, T, D), bf16),
                pltpu.VMEM((2, T, heads * D), bf16),
                pltpu.VMEM((2, T, heads * D), bf16),
                dma((4,)),
                dma(((reach + 1) * 4,)),
                dma(((reach + 1) * 4,)),
                dma((2,)),
                dma((2,)),
                dma((reach * 4,)),
                dma(((reach + 1) * 2,)),
                dma(((reach + 1) * 2,)),
                dma((reach * 2,)),
                dma((reach * 2,)),
                dma((2,)),
                dma((2,)),
                dma((2,)),
            ],
            compiler_params=pltpu.CompilerParams(
                collective_id=0, has_side_effects=True, vmem_limit_bytes=VMEM_LIMIT
            ),
        )(queries, out_grad, key_states, value_states, doc_lengths)
        return pl.pallas_call(
            place_results,
            out_shape=tuple(jax.ShapeDtypeStruct(x.shape, x.dtype) for x in results),
            in_specs=[hbm] * 4,
            out_specs=(hbm,) * 4,
            scratch_shapes=[pltpu.VMEM(x.shape, x.dtype) for x in results] + [dma((4,)), dma((4,))],
            compiler_params=pltpu.CompilerParams(vmem_limit_bytes=VMEM_LIMIT),
        )(*results)

    return jax.shard_map(
        body,
        mesh=mesh,
        in_specs=(P(("ctx", "kv"), None),) * 4 + (P(),),
        out_specs=(P(("ctx", "kv"), None),) * 4,
        check_vma=False,
    )
```
